32 devices in a mesh: section: 8 (over y, x, core), dp: 4 (over z).
Axes of the slice: x: 2, y: 2, z: 4, core: 2. Of those that a mesh axis runs over, the one named last changes fastest.
Arguments:
- inputs: bfloat16 [8, 2, 1024, 2048], P('section', None, 'dp'), may hold values from -6 to 6
- cotangent: bfloat16 [8, 2, 1024, 2048], P('section', None, 'dp'), may hold values from -6 to 6
- w_gate: bfloat16 [8, 2, 2048, 256], P('section'), may hold values from -0.125 to 0.125
- w_up: bfloat16 [8, 2, 2048, 256], P('section'), may hold values from -0.125 to 0.125
- w_down: bfloat16 [8, 2, 256, 2048], P('section'), may hold values from -0.375 to 0.375
- mom_gate: float32 [8, 2048, 256], P('section', 'dp'), may hold values from -6 to 6
- mom_up: float32 [8, 2048, 256], P('section', 'dp'), may hold values from -6 to 6
- mom_down: float32 [8, 2048, 256], P('section', 'dp'), may hold values from -6 to 6
Outputs:
- grad_in: bfloat16 [8, 2, 1024, 2048], P('section', None, 'dp')
- new_gate: float32 [8, 2048, 256], P('section', 'dp')
- new_up: float32 [8, 2048, 256], P('section', 'dp')
- new_down: float32 [8, 2048, 256], P('section', 'dp')
The draws below stay inside these ranges and needn't reach their ends.
All inputs are finite; a program needn't handle non-finite values.
Results may differ from the reference program's by a relative error of at most 0.009.
Values may be sent and summed in bfloat16 or wider, within the bound.
No kernel may reach another device: no remote copies, remote signals or barrier semaphores. Data moves between devices by JAX's collectives and lax.ppermute only.
A program may use at most 128 MiB of HBM per device.

```python
import jax
import jax.numpy as jnp
from jax import lax

D = 2048
FF = 256
TOK_DEV = 256
TOKENS = 1024
N_SECTION = 8
N_DP = 4


def spiked(values, rng, source, target, parts, factor):
    owner, partner = [(jnp.arange(values.shape[axis_at]) // (values.shape[axis_at] // parts)).reshape([-1 if axis == axis_at else 1 for axis in range(values.ndim)]) for axis_at in (source, target)]
    chosen = jax.random.permutation(rng, parts)[partner]
    strong = (owner == chosen) | (owner == (partner + parts // 2) % parts)
    return jnp.where(strong, factor * values, values)


def block_scale(own_key, dims, cuts, least, high):
    factor_of, own = 1.0, jax.random.fold_in(own_key, 6)
    for position, shards_of in cuts:
        steps = jnp.exp(jax.random.uniform(jax.random.fold_in(own, position), (shards_of,), jnp.float32, least / len(cuts), high / len(cuts)))
        factor_of = factor_of * jnp.repeat(steps, dims[position] // shards_of).reshape([-1 if axis == position else 1 for axis in range(len(dims))])
    return factor_of


def gaussian(rng, dims, spread, limit, pieces=(), held_as=jnp.bfloat16):
    drawn = spread * jax.random.normal(rng, dims, jnp.float32)
    if pieces:
        drawn = drawn * block_scale(rng, dims, pieces, -0.22, 0.18)
    return jnp.clip(drawn, -limit, limit).astype(held_as)


def gaussian_with(key, extent, width, bound, pieces, heavy, kind=jnp.bfloat16):
    drawn = width * jax.random.normal(key, extent, jnp.float32)
    if pieces:
        drawn = drawn * block_scale(key, extent, pieces, -0.22, 0.18)
    return jnp.clip(spiked(drawn, jax.random.fold_in(key, 3), *heavy), -bound, bound).astype(kind)


def setup_inputs(seed: int = 0) -> dict:
    streams_of = jax.random.split(jax.random.key(seed), 9)
    inputs = gaussian_with(streams_of[0], (N_SECTION, 2, TOKENS, D), 1.0, 6.0, ((0, 8), (2, 4)), (2, 3, 4, 2.0))
    cotangent = gaussian_with(streams_of[1], (N_SECTION, 2, TOKENS, D), 1.0, 6.0, ((0, 8), (2, 4)), (2, 3, 4, 2.0))
    w_gate = gaussian(streams_of[2], (N_SECTION, 2, D, FF), D ** -0.5, 0.125, ((0, 8),))
    w_up = gaussian(streams_of[3], (N_SECTION, 2, D, FF), D ** -0.5, 0.125, ((0, 8),))
    w_down = gaussian(streams_of[4], (N_SECTION, 2, FF, D), FF ** -0.5, 0.375, ((0, 8),))
    mom_gate = gaussian(streams_of[5], (N_SECTION, D, FF), 1.0, 6.0, ((0, 8), (1, 4)), jnp.float32)
    mom_up = gaussian(streams_of[6], (N_SECTION, D, FF), 1.0, 6.0, ((0, 8), (1, 4)), jnp.float32)
    mom_down = gaussian(streams_of[7], (N_SECTION, D, FF), 1.0, 6.0, ((0, 8), (1, 4)), jnp.float32)
    return dict(inputs=inputs, cotangent=cotangent, w_gate=w_gate, w_up=w_up, w_down=w_down, mom_gate=mom_gate, mom_up=mom_up, mom_down=mom_down)


def backward_block(block_in, block_cot, gate_mat, up_mat, down_mat):
    gate_pre = jnp.dot(block_in, gate_mat, preferred_element_type=jnp.float32)
    up_pre = jnp.dot(block_in, up_mat, preferred_element_type=jnp.float32)
    sigmoid_val = jax.nn.sigmoid(gate_pre)
    activated = gate_pre * sigmoid_val
    hidden = (activated * up_pre).astype(jnp.bfloat16)
    hidden_grad = jnp.dot(block_cot, down_mat.T, preferred_element_type=jnp.float32)
    gate_grad = (hidden_grad * up_pre * sigmoid_val * (1.0 + gate_pre * (1.0 - sigmoid_val))).astype(jnp.bfloat16)
    up_grad = (hidden_grad * activated).astype(jnp.bfloat16)
    input_grad = (jnp.dot(gate_grad, gate_mat.T, preferred_element_type=jnp.float32) + jnp.dot(up_grad, up_mat.T, preferred_element_type=jnp.float32)).astype(jnp.bfloat16)
    return (input_grad, gate_grad, up_grad, hidden)

def replica_grads(block_in, block_cot, gate_grad, up_grad, hidden):
    groups_in = block_in.reshape(N_DP, TOK_DEV, D).astype(jnp.float32)
    groups_cot = block_cot.reshape(N_DP, TOK_DEV, D).astype(jnp.float32)
    groups_gate = gate_grad.reshape(N_DP, TOK_DEV, FF).astype(jnp.float32)
    groups_up = up_grad.reshape(N_DP, TOK_DEV, FF).astype(jnp.float32)
    groups_hid = hidden.reshape(N_DP, TOK_DEV, FF).astype(jnp.float32)
    part_gate = jnp.einsum('gtd,gtf->gdf', groups_in, groups_gate)
    part_up = jnp.einsum('gtd,gtf->gdf', groups_in, groups_up)
    part_down = jnp.einsum('gtd,gtf->gdf', groups_cot, groups_hid)
    return jnp.stack([part_gate, part_up, part_down])

def per_section(packed):
    section_in, section_cot, section_gate, section_up, section_down = packed
    first = backward_block(section_in[0], section_cot[0], section_gate[0], section_up[0], section_down[0])
    second = backward_block(section_in[1], section_cot[1], section_gate[1], section_up[1], section_down[1])
    parts_first = replica_grads(section_in[0], section_cot[0], first[1], first[2], first[3])
    parts_second = replica_grads(section_in[1], section_cot[1], second[1], second[2], second[3])
    rounded = lax.optimization_barrier(parts_second.astype(jnp.bfloat16)).astype(jnp.float32)
    return (jnp.stack([first[0], second[0]]), lax.optimization_barrier(jnp.sum(parts_first, axis=1)), lax.optimization_barrier(jnp.sum(rounded, axis=1)))

def reference(inputs, cotangent, w_gate, w_up, w_down, mom_gate, mom_up, mom_down):
    input_grads, grads_first, grads_second = lax.map(per_section, (inputs, cotangent, w_gate, w_up, w_down))
    zero_rows = jnp.zeros((1, TOKENS, D), jnp.bfloat16)
    recv_first = jnp.concatenate([input_grads[1:, 0], zero_rows], axis=0)
    recv_second = jnp.concatenate([zero_rows, input_grads[:-1, 1]], axis=0)
    grad_in = jnp.stack([recv_first, recv_second], axis=1)
    combined = grads_first + jnp.flip(grads_second, axis=0)
    scale_factor = 1.0 / jnp.sqrt(jnp.float32(TOKENS))
    new_gate = 0.9 * mom_gate + combined[:, 0] * scale_factor
    new_up = 0.9 * mom_up + combined[:, 1] * scale_factor
    new_down = 0.9 * mom_down + combined[:, 2] * scale_factor
    return (grad_in, new_gate, new_up, new_down)
```

```python
import functools
import math

import jax
import jax.numpy as jnp
from jax import lax
from jax.experimental import pallas as pl
from jax.experimental.pallas import tpu as pltpu
from jax.sharding import PartitionSpec as P

BF16 = jnp.bfloat16
F32 = jnp.float32
VMEM_LIMIT = 48 * 1024 * 1024


def rows_dot(left, right):
    return lax.dot_general(left, right, (((0,), (0,)), ((), ())), preferred_element_type=F32)


def cols_dot(left, right):
    return lax.dot_general(left, right, (((1,), (1,)), ((), ())), preferred_element_type=F32)


def slot_offsets(count):
    bits = count.bit_length() - 1
    return [sum(((p >> i) & 1) << (bits - 1 - i) for i in range(bits)) for p in range(count)]


def block_kernel(offsets, shard, mine, x_ref, y_ref, wg_ref, wu_ref, wd_ref, dgu_ref, pd_ref, dx_ref):
    ff = wg_ref.shape[3]
    x, y = x_ref[0, 0], y_ref[0, 0]
    gate = jnp.dot(x, wg_ref[0, 0], preferred_element_type=F32)
    up = jnp.dot(x, wu_ref[0, 0], preferred_element_type=F32)
    sig = jax.nn.sigmoid(gate)
    act = gate * sig
    hidden = (act * up).astype(BF16)
    dhid = cols_dot(y, wd_ref[0, 0])
    dgate = (dhid * up * sig * (1.0 + gate * (1.0 - sig))).astype(BF16)
    dup = (dhid * act).astype(BF16)
    dgu_ref[0, :, :ff] = dgate
    dgu_ref[0, :, ff:] = dup
    hidden_t = hidden.T
    for slot, offset in enumerate(offsets):
        start = pl.multiple_of((mine[0] ^ offset) * shard, shard)
        columns = y_ref[0, 0, :, pl.ds(start, shard)]
        pd_ref[0, slot] = jnp.dot(hidden_t, columns, preferred_element_type=F32).astype(BF16)
    width = x_ref.shape[3]
    step = min(512, width)
    for at in range(0, width, step):
        rows = pl.ds(at, step)
        dx_ref[0, :, rows] = (
            cols_dot(dgate, wg_ref[0, 0, rows, :]) + cols_dot(dup, wu_ref[0, 0, rows, :])
        ).astype(BF16)


def blocks(mine, inputs, cotangent, w_gate, w_up, w_down, offsets, shard):
    _, _, rows, width = inputs.shape
    ff = w_gate.shape[3]
    count = len(offsets)
    whole = lambda b, z: (0, b, 0, 0)
    return pl.pallas_call(
        functools.partial(block_kernel, offsets, shard),
        out_shape=(
            jax.ShapeDtypeStruct((2, rows, 2 * ff), BF16),
            jax.ShapeDtypeStruct((2, count, ff, shard), BF16),
            jax.ShapeDtypeStruct((2, rows, width), BF16),
        ),
        grid_spec=pltpu.PrefetchScalarGridSpec(
            num_scalar_prefetch=1,
            grid=(2,),
            in_specs=[
                pl.BlockSpec((1, 1, rows, width), whole),
                pl.BlockSpec((1, 1, rows, width), whole),
                pl.BlockSpec((1, 1, width, ff), whole),
                pl.BlockSpec((1, 1, width, ff), whole),
                pl.BlockSpec((1, 1, ff, width), whole),
            ],
            out_specs=[
                pl.BlockSpec((1, rows, 2 * ff), lambda b, z: (b, 0, 0)),
                pl.BlockSpec((1, count, ff, shard), lambda b, z: (b, 0, 0, 0)),
                pl.BlockSpec((1, rows, width), lambda b, z: (b, 0, 0)),
            ],
        ),
        compiler_params=pltpu.CompilerParams(vmem_limit_bytes=VMEM_LIMIT),
        name="blocks",
    )(mine, inputs, cotangent, w_gate, w_up, w_down)


def pair_kernel(mine, x0_ref, x1_ref, d0_ref, d1_ref, gate_ref, up_ref):
    ff = gate_ref.shape[1]
    x0, x1 = x0_ref[0, 0], x1_ref[0]
    for out, at in ((gate_ref, 0), (up_ref, ff)):
        out[0] = (rows_dot(d0_ref[0, :, at : at + ff], x0) + rows_dot(d1_ref[:, at : at + ff], x1)).astype(BF16)


def pair(mine, inputs, mirrored_x, dgu, mirrored_dgu, offsets, shard):
    _, _, rows, _ = inputs.shape
    ff = dgu.shape[2] // 2
    count = len(offsets)

    def column(j, z):
        offset = sum(jnp.where(j == i, o, 0) for i, o in enumerate(offsets))
        return (0, 0, 0, z[0] ^ offset)

    return pl.pallas_call(
        pair_kernel,
        out_shape=(jax.ShapeDtypeStruct((count, ff, shard), BF16),) * 2,
        grid_spec=pltpu.PrefetchScalarGridSpec(
            num_scalar_prefetch=1,
            grid=(count,),
            in_specs=[
                pl.BlockSpec((1, 1, rows, shard), column),
                pl.BlockSpec((1, rows, shard), lambda j, z: (j, 0, 0)),
                pl.BlockSpec((1, rows, 2 * ff), lambda j, z: (0, 0, 0)),
                pl.BlockSpec((rows, 2 * ff), lambda j, z: (0, 0)),
            ],
            out_specs=[pl.BlockSpec((1, ff, shard), lambda j, z: (j, 0, 0))] * 2,
        ),
        compiler_params=pltpu.CompilerParams(vmem_limit_bytes=VMEM_LIMIT),
        name="pair",
    )(mine, inputs, mirrored_x, dgu, mirrored_dgu)


def momentum_kernel(scale, mom_ref, *refs):
    out_ref = refs[-1]
    total = refs[0][0].astype(F32)
    for ref in refs[1:-1]:
        total = total + ref[0].astype(F32)
    out_ref[0] = 0.9 * mom_ref[0] + total.T * scale


def momentum(mom, parts, scale):
    _, shard, ff = mom.shape
    return pl.pallas_call(
        functools.partial(momentum_kernel, scale),
        out_shape=jax.ShapeDtypeStruct(mom.shape, F32),
        grid=(1,),
        in_specs=[pl.BlockSpec((1, shard, ff), lambda i: (0, 0, 0))]
        + [pl.BlockSpec((1, ff, shard), lambda i: (0, 0, 0))] * len(parts),
        out_specs=pl.BlockSpec((1, shard, ff), lambda i: (0, 0, 0)),
        compiler_params=pltpu.CompilerParams(vmem_limit_bytes=VMEM_LIMIT),
        name="momentum",
    )(mom, *parts)


def shifted(value, steps):
    count = lax.axis_size("section")
    first, last = max(0, -steps), min(count, count - steps)
    return lax.ppermute(value, "section", [(i, i + steps) for i in range(first, last)])


def mirrored(value):
    count = lax.axis_size("section")
    return lax.ppermute(value, "section", [(i, count - 1 - i) for i in range(count)])


def swapped(value, mask):
    return lax.ppermute(value, "dp", [(i, i ^ mask) for i in range(lax.axis_size("dp"))])


def halve(keep, received):
    half = keep.shape[0] // 2
    add = lambda a, b: (a.astype(F32) + b.astype(F32)).astype(BF16)
    return keep[:half], received[:half], add(keep[half:], received[half:])


def body(inputs, cotangent, w_gate, w_up, w_down, mom_gate, mom_up, mom_down):
    replicas = lax.axis_size("dp")
    _, _, rows, width = inputs.shape
    shard = width // replicas
    offsets = slot_offsets(replicas)
    half = replicas // 2
    z = lax.axis_index("dp")
    mine = z[None]
    scale = 1.0 / math.sqrt(rows * replicas)

    def columns(value, chosen):
        return jnp.stack([lax.dynamic_slice_in_dim(value, (z ^ o) * shard, shard, 1) for o in chosen])

    x_send = mirrored(columns(inputs[0, 1], offsets[half:]))
    dgu, pd, dx = blocks(mine, inputs, cotangent, w_gate, w_up, w_down, offsets, shard)
    dgu_mirror = mirrored(dgu[1])
    x_keep = mirrored(columns(inputs[0, 1], offsets[:half]))
    pd_mirror = mirrored(pd[1])
    add = lambda a, b: (a.astype(F32) + b.astype(F32)).astype(BF16)
    gate_send, up_send = pair(mine, inputs, x_send, dgu, dgu_mirror, offsets[half:], shard)
    gate_keep, up_keep = pair(mine, inputs, x_keep, dgu, dgu_mirror, offsets[:half], shard)
    down_send = add(pd[0, half:], pd_mirror[half:])
    down_keep = add(pd[0, :half], pd_mirror[:half])
    recv0 = shifted(dx[0], -1)
    recv1 = shifted(dx[1], 1)
    results = []
    for mom, keep, send in (
        (mom_gate, gate_keep, gate_send),
        (mom_up, up_keep, up_send),
        (mom_down, down_keep, down_send),
    ):
        mask = 1
        while mask < replicas:
            received = swapped(send, mask)
            m = keep.shape[0] // 2
            if m:
                send = add(keep[m:], received[m:])
                keep = add(keep[:m], received[:m])
            else:
                results.append(momentum(mom, (keep, received), scale))
            mask *= 2
    grad_in = jnp.stack([recv0, recv1])[None]
    return (grad_in, *results)


def solution(mesh):
    tokens = P("section", None, "dp", None)
    weights = P("section", None, None, None)
    moments = P("section", "dp", None)
    return jax.shard_map(
        body,
        mesh=mesh,
        in_specs=(tokens, tokens, weights, weights, weights, moments, moments, moments),
        out_specs=(tokens, moments, moments, moments),
        check_vma=False,
    )
```

```python
import functools
import math

import jax
import jax.numpy as jnp
from jax import lax
from jax.experimental import pallas as pl
from jax.experimental.pallas import tpu as pltpu
from jax.sharding import PartitionSpec as P

BF16 = jnp.bfloat16
F32 = jnp.float32
VMEM_LIMIT = 8 * 1024 * 1024
COST = pl.CostEstimate(flops=1000, bytes_accessed=1000, transcendentals=0)


def rows_dot(left, right):
    return lax.dot_general(left, right, (((0,), (0,)), ((), ())), preferred_element_type=F32)


def cols_dot(left, right):
    return lax.dot_general(left, right, (((1,), (1,)), ((), ())), preferred_element_type=F32)


def slot_offsets(count, masks):
    offsets = [0]
    for mask in reversed(masks):
        offsets = offsets + [o ^ mask for o in offsets]
    return offsets


def columns_of(mine, offset, shard):
    return pl.ds(pl.multiple_of((mine[0] ^ offset) * shard, shard), shard)


def activations_kernel(cut, mine, *refs):
    sources, outs, held, made = refs[:5], refs[5:11], refs[11:16], refs[16:19]
    in_sems, out_sems = refs[19:]
    dgu_out, x_send_out, x_keep_out, hidden_out, send_out = outs[0:2], *outs[2:6]
    dgu_ref, hidden_ref, send_ref = made
    copies = {}

    def read(b):
        for i in (0, 2, 3, 1, 4):
            copies[b, i] = pltpu.make_async_copy(sources[i].at[0, b], held[i].at[b], in_sems.at[b, i])
            copies[b, i].start()

    written = []

    def write(source, target):
        copy = pltpu.make_async_copy(source, target, out_sems.at[len(written)])
        copy.start()
        written.append(copy)

    read(1)
    for b in (1, 0):
        x_ref, y_ref, wg_ref, wu_ref, wd_ref = (ref.at[b] for ref in held)
        half, ff, shard = send_ref.shape[1:]
        copies[b, 0].wait()
        copies[b, 2].wait()
        gate = jnp.dot(x_ref[...], wg_ref[...], preferred_element_type=F32)
        copies[b, 3].wait()
        up = jnp.dot(x_ref[...], wu_ref[...], preferred_element_type=F32)
        copies[b, 1].wait()
        copies[b, 4].wait()
        if b:
            read(0)
            for slot, offset in enumerate(cut):
                target = x_keep_out if slot < half else x_send_out
                write(x_ref.at[:, columns_of(mine, offset, shard)], target.at[slot % half])
        dhid = cols_dot(y_ref[...], wd_ref[...])
        sig = jax.nn.sigmoid(gate)
        act = gate * sig
        hidden = (act * up).astype(BF16)
        dgu_ref[b, :, :ff] = (dhid * up * sig * (1.0 + gate * (1.0 - sig))).astype(BF16)
        dgu_ref[b, :, ff:] = (dhid * act).astype(BF16)
        write(dgu_ref.at[b], dgu_out[b])
        hidden_ref[b] = hidden
        hidden_t = hidden.T
        for slot in range(half):
            columns = y_ref[:, columns_of(mine, cut[half + slot], shard)]
            send_ref[b, slot] = jnp.dot(hidden_t, columns, preferred_element_type=F32).astype(BF16)
        write(send_ref.at[b], send_out.at[b])
    write(hidden_ref, hidden_out)
    for copy in written:
        copy.wait()


def activations(mine, inputs, cotangent, w_gate, w_up, w_down, cut, shard):
    _, _, rows, width = inputs.shape
    ff = w_gate.shape[3]
    half = len(cut) // 2
    outs = [(rows, 2 * ff)] * 2 + [(half, rows, shard)] * 2 + [(2, rows, ff), (2, half, ff, shard)]
    made = [(2, rows, 2 * ff), (2, rows, ff), (2, half, ff, shard)]
    return pl.pallas_call(
        functools.partial(activations_kernel, cut),
        out_shape=tuple(jax.ShapeDtypeStruct(dims, BF16) for dims in outs),
        in_specs=[pl.BlockSpec(memory_space=pltpu.SMEM)] + [pl.BlockSpec(memory_space=pl.ANY)] * 5,
        out_specs=[pl.BlockSpec(memory_space=pl.ANY)] * len(outs),
        scratch_shapes=[pltpu.VMEM((2, *array.shape[2:]), BF16) for array in (inputs, cotangent, w_gate, w_up, w_down)]
        + [pltpu.VMEM(dims, BF16) for dims in made]
        + [pltpu.SemaphoreType.DMA((2, 5)), pltpu.SemaphoreType.DMA((len(cut) + 5,))],
        compiler_params=pltpu.CompilerParams(vmem_limit_bytes=48 * 1024 * 1024),
        name="activations",
    )(mine, inputs, cotangent, w_gate, w_up, w_down)


def rest_kernel(cut, mine, y_ref, wg_ref, wu_ref, dgu0_ref, dgu1_ref, hidden_ref, keep_ref, dx_ref):
    half, ff, shard = keep_ref.shape[1:]
    width = y_ref.shape[3]
    hidden_t = hidden_ref[0].T
    for slot in range(half):
        columns = y_ref[0, 0, :, columns_of(mine, cut[slot], shard)]
        keep_ref[0, slot] = jnp.dot(hidden_t, columns, preferred_element_type=F32).astype(BF16)
    first = pl.program_id(0) == 0
    dgu = jnp.where(first, dgu0_ref[...], dgu1_ref[...])
    dgate, dup = dgu[:, :ff], dgu[:, ff:]
    step = min(512, width)
    for start in range(0, width, step):
        rows = pl.ds(start, step)
        dx_ref[0, :, rows] = (
            cols_dot(dgate, wg_ref[0, 0, rows, :]) + cols_dot(dup, wu_ref[0, 0, rows, :])
        ).astype(BF16)


def rest(mine, cotangent, w_gate, w_up, dgu0, dgu1, hidden, cut, shard):
    _, _, rows, width = cotangent.shape
    ff = w_gate.shape[3]
    half = len(cut) // 2
    whole = lambda b, z: (0, b, 0, 0)
    return pl.pallas_call(
        functools.partial(rest_kernel, cut),
        out_shape=(
            jax.ShapeDtypeStruct((2, half, ff, shard), BF16),
            jax.ShapeDtypeStruct((2, rows, width), BF16),
        ),
        grid_spec=pltpu.PrefetchScalarGridSpec(
            num_scalar_prefetch=1,
            grid=(2,),
            in_specs=[
                pl.BlockSpec((1, 1, rows, width), whole),
                pl.BlockSpec((1, 1, width, ff), whole),
                pl.BlockSpec((1, 1, width, ff), whole),
                pl.BlockSpec((rows, 2 * ff), lambda b, z: (0, 0)),
                pl.BlockSpec((rows, 2 * ff), lambda b, z: (0, 0)),
                pl.BlockSpec((1, rows, ff), lambda b, z: (b, 0, 0)),
            ],
            out_specs=[
                pl.BlockSpec((1, half, ff, shard), lambda b, z: (b, 0, 0, 0)),
                pl.BlockSpec((1, rows, width), lambda b, z: (b, 0, 0)),
            ],
        ),
        compiler_params=pltpu.CompilerParams(vmem_limit_bytes=48 * 1024 * 1024),
        cost_estimate=COST,
        name="rest",
    )(mine, cotangent, w_gate, w_up, dgu0, dgu1, hidden)


def pair_kernel(mine, x0_ref, x1_ref, d0_ref, d1_ref, out_ref):
    out_ref[0] = (rows_dot(d0_ref[...], x0_ref[0, 0]) + rows_dot(d1_ref[...], x1_ref[0])).astype(BF16)


def pair(mine, inputs, mirrored_x, dgu, mirrored_dgu, offsets, shard):
    _, _, rows, _ = inputs.shape
    both = dgu.shape[1]
    count = len(offsets)

    def column(j, z):
        offset = sum(jnp.where(j == i, o, 0) for i, o in enumerate(offsets))
        return (0, 0, 0, z[0] ^ offset)

    return pl.pallas_call(
        pair_kernel,
        out_shape=jax.ShapeDtypeStruct((count, both, shard), BF16),
        grid_spec=pltpu.PrefetchScalarGridSpec(
            num_scalar_prefetch=1,
            grid=(count,),
            in_specs=[
                pl.BlockSpec((1, 1, rows, shard), column),
                pl.BlockSpec((1, rows, shard), lambda j, z: (j, 0, 0)),
                pl.BlockSpec((rows, both), lambda j, z: (0, 0)),
                pl.BlockSpec((rows, both), lambda j, z: (0, 0)),
            ],
            out_specs=pl.BlockSpec((1, both, shard), lambda j, z: (j, 0, 0)),
        ),
        compiler_params=pltpu.CompilerParams(vmem_limit_bytes=VMEM_LIMIT),
        cost_estimate=COST,
        name="pair",
    )(mine, inputs, mirrored_x, dgu, mirrored_dgu)


def momentum_kernel(scale, count, *refs):
    moms, parts, outs = refs[:count], refs[count:-count], refs[-count:]
    ff = moms[0].shape[2]
    for i in range(count):
        total = parts[0][0, i * ff : (i + 1) * ff].astype(F32)
        for ref in parts[1:]:
            total = total + ref[0, i * ff : (i + 1) * ff].astype(F32)
        outs[i][0] = 0.9 * moms[i][0] + total.T * scale


def momentum(moms, parts, scale):
    shape = moms[0].shape
    _, shard, ff = shape
    count = len(moms)
    whole = pl.BlockSpec((1, shard, ff), lambda i: (0, 0, 0))
    return pl.pallas_call(
        functools.partial(momentum_kernel, scale, count),
        out_shape=(jax.ShapeDtypeStruct(shape, F32),) * count,
        grid=(1,),
        in_specs=[whole] * count + [pl.BlockSpec((1, ff * count, shard), lambda i: (0, 0, 0))] * len(parts),
        out_specs=[whole] * count,
        compiler_params=pltpu.CompilerParams(vmem_limit_bytes=2 * VMEM_LIMIT),
        cost_estimate=COST,
        name="momentum",
    )(*moms, *parts)


def shifted(value, steps, name):
    count = lax.axis_size("section")
    first, last = max(0, -steps), min(count, count - steps)
    with jax.named_scope(name):
        return lax.ppermute(value, "section", [(i, i + steps) for i in range(first, last)])


def mirrored(value, name):
    count = lax.axis_size("section")
    with jax.named_scope(name):
        return lax.ppermute(value, "section", [(i, count - 1 - i) for i in range(count)])


def swapped(value, mask, name):
    with jax.named_scope(name):
        return lax.ppermute(value, "dp", [(i, i ^ mask) for i in range(lax.axis_size("dp"))])


def after(value, earlier):
    return lax.optimization_barrier((value, earlier))[0]


def add(left, right):
    return (left.astype(F32) + right.astype(F32)).astype(BF16)


def finish(keep, received, masks, name, axis):
    for mask in masks[1:]:
        (stay, go), (stayed, gone) = (jnp.split(v, 2, axis) for v in (keep, received))
        keep = add(stay, stayed)
        received = swapped(add(go, gone), mask, name)
    return keep, received


def body(inputs, cotangent, w_gate, w_up, w_down, mom_gate, mom_up, mom_down):
    replicas = lax.axis_size("dp")
    _, _, rows, width = inputs.shape
    shard = width // replicas
    half = replicas // 2
    masks = [1 << i for i in range(replicas.bit_length() - 1)]
    cut = slot_offsets(replicas, masks)
    mine = lax.axis_index("dp")[None]
    scale = 1.0 / math.sqrt(rows * replicas)

    dgu0, dgu1, x_send, x_keep, hidden, down_send = activations(
        mine, inputs, cotangent, w_gate, w_up, w_down, cut, shard
    )
    down_keep, dx = rest(mine, cotangent, w_gate, w_up, dgu0, dgu1, hidden, cut, shard)
    x_send, dgu1 = mirrored(x_send, "x_send"), mirrored(dgu1, "dgu")
    down_first = swapped(down_send, masks[0], "down_first")
    x_keep = mirrored(x_keep, "x_keep")
    recv0 = shifted(after(dx[0], x_keep), -1, "dx_first")
    recv1 = shifted(after(dx[1], x_keep), 1, "dx_second")
    pair_send = pair(mine, inputs, x_send, dgu0, dgu1, cut[half:], shard)
    pair_first = swapped(pair_send, masks[0], "pair_first")
    down_keep, down_last = finish(down_keep, down_first, masks, "down_rest", 1)
    mirror = add(down_keep[1], down_last[1])
    mirror = mirrored(after(mirror, (recv0, recv1)), "down_mirror")
    pair_keep = pair(mine, inputs, x_keep, dgu0, dgu1, cut[:half], shard)
    pair_parts = finish(pair_keep, pair_first, masks, "pair_rest", 0)
    new_down = momentum([mom_down], (down_keep[0], down_last[0], mirror), scale)
    results = [*momentum([mom_gate, mom_up], pair_parts, scale), *new_down]
    grad_in = jnp.stack([recv0, recv1])[None]
    return (grad_in, *results)


def solution(mesh):
    tokens = P("section", None, "dp", None)
    weights = P("section", None, None, None)
    moments = P("section", "dp", None)
    return jax.shard_map(
        body,
        mesh=mesh,
        in_specs=(tokens, tokens, weights, weights, weights, moments, moments, moments),
        out_specs=(tokens, moments, moments, moments),
        check_vma=False,
    )
```

```python
import functools
import math

import jax
import jax.numpy as jnp
from jax import lax
from jax.experimental import pallas as pl
from jax.experimental.pallas import tpu as pltpu
from jax.sharding import PartitionSpec as P

BF16 = jnp.bfloat16
F32 = jnp.float32
VMEM_LIMIT = 8 * 1024 * 1024
SECOND_LIMIT = 58 * 1024 * 1024
REST_LIMIT = 48 * 1024 * 1024
COST = pl.CostEstimate(flops=1000, bytes_accessed=1000, transcendentals=0)
LONG = pl.CostEstimate(flops=1000, bytes_accessed=10**9, transcendentals=0)


def rows_dot(left, right):
    return lax.dot_general(left, right, (((0,), (0,)), ((), ())), preferred_element_type=F32)


def cols_dot(left, right):
    return lax.dot_general(left, right, (((1,), (1,)), ((), ())), preferred_element_type=F32)


def slot_offsets(count, masks):
    offsets = [0]
    for mask in reversed(masks):
        offsets = offsets + [o ^ mask for o in offsets]
    return offsets


def columns_of(mine, offset, shard):
    return pl.ds(pl.multiple_of((mine[0] ^ offset) * shard, shard), shard)


def reader(pairs, sems):
    copies = [pltpu.make_async_copy(source, target, sems.at[i]) for i, (source, target) in enumerate(pairs)]
    for copy in copies:
        copy.start()
    return copies


def backward(gate, up, dhid):
    sig = jax.nn.sigmoid(gate)
    act = gate * sig
    hidden = (act * up).astype(BF16)
    return hidden, (dhid * up * sig * (1.0 + gate * (1.0 - sig))).astype(BF16), (dhid * act).astype(BF16)


def slots_into(out_ref, mine, offsets, hidden_t, y_ref):
    shard = out_ref.shape[2]
    for slot, offset in enumerate(offsets):
        columns = y_ref[:, columns_of(mine, offset, shard)]
        out_ref[slot] = jnp.dot(hidden_t, columns, preferred_element_type=F32).astype(BF16)


def second_kernel(cut, mine, x_hbm, y_hbm, wg_hbm, wu_hbm, wd_hbm, dgu_ref, hidden_ref, send_ref, x_send_ref, x_keep_ref, *held):
    (x_ref, wg_ref, wu_ref, y_ref, wd_ref), sems, slot_sems = held[:5], held[5], held[6]
    half, ff, shard = send_ref.shape
    hbm = (x_hbm, wg_hbm, wu_hbm, y_hbm, wd_hbm)
    copies = reader([(source.at[0, 1], target) for source, target in zip(hbm, held)], sems)
    copies[0].wait()
    slots = reader(
        [
            (x_ref.at[:, columns_of(mine, offset, shard)], (x_keep_ref if i < half else x_send_ref).at[i % half])
            for i, offset in enumerate(cut)
        ],
        slot_sems,
    )
    copies[1].wait()
    gate = jnp.dot(x_ref[...], wg_ref[...], preferred_element_type=F32)
    copies[2].wait()
    up = jnp.dot(x_ref[...], wu_ref[...], preferred_element_type=F32)
    copies[3].wait()
    copies[4].wait()
    dhid = cols_dot(y_ref[...], wd_ref[...])
    hidden, dgate, dup = backward(gate, up, dhid)
    dgu_ref[:, :ff] = dgate
    dgu_ref[:, ff:] = dup
    hidden_ref[...] = hidden
    slots_into(send_ref, mine, cut[half:], hidden.T, y_ref)
    for copy in slots:
        copy.wait()


def second(mine, inputs, cotangent, w_gate, w_up, w_down, cut, shard):
    _, _, rows, width = inputs.shape
    ff = w_gate.shape[3]
    half = len(cut) // 2
    outs = [(rows, 2 * ff), (rows, ff), (half, ff, shard), (half, rows, shard), (half, rows, shard)]
    return pl.pallas_call(
        functools.partial(second_kernel, cut),
        out_shape=tuple(jax.ShapeDtypeStruct(dims, BF16) for dims in outs),
        in_specs=[pl.BlockSpec(memory_space=pltpu.SMEM)] + [pl.BlockSpec(memory_space=pl.ANY)] * 5,
        out_specs=[pl.BlockSpec(memory_space=pltpu.VMEM)] * len(outs),
        scratch_shapes=[pltpu.VMEM(array.shape[2:], BF16) for array in (inputs, w_gate, w_up, cotangent, w_down)]
        + [pltpu.SemaphoreType.DMA((5,)), pltpu.SemaphoreType.DMA((len(cut),))],
        compiler_params=pltpu.CompilerParams(vmem_limit_bytes=SECOND_LIMIT),
        cost_estimate=LONG,
        name="second",
    )(mine, inputs, cotangent, w_gate, w_up, w_down)


def rest_kernel(cut, mine, x_hbm, y_hbm, wg_hbm, wu_hbm, wd_hbm, dgu1_ref, hidden1_ref, *refs):
    dgu_ref, send_ref, keep0_ref, keep1_ref, dx0_ref, dx1_ref = refs[:6]
    (x_ref, wg_ref, wu_ref, y_ref, wd_ref, y1_ref, wg1_ref, wu1_ref), sems = refs[6:14], refs[14]
    half, ff, shard = send_ref.shape
    width = x_ref.shape[1]
    hbm = (x_hbm, wg_hbm, wu_hbm, y_hbm, wd_hbm)
    sources = [source.at[0, 0] for source in hbm] + [source.at[0, 1] for source in (y_hbm, wg_hbm, wu_hbm)]
    copies = reader(list(zip(sources, refs[6:14])), sems)

    def input_gradient(out_ref, dgate, dup, wg, wu):
        step = min(512, width)
        for start in range(0, width, step):
            rows = pl.ds(start, step)
            out_ref[:, rows] = (cols_dot(dgate, wg[rows, :]) + cols_dot(dup, wu[rows, :])).astype(BF16)

    copies[0].wait()
    copies[1].wait()
    gate = jnp.dot(x_ref[...], wg_ref[...], preferred_element_type=F32)
    copies[2].wait()
    up = jnp.dot(x_ref[...], wu_ref[...], preferred_element_type=F32)
    copies[3].wait()
    copies[4].wait()
    hidden, dgate, dup = backward(gate, up, cols_dot(y_ref[...], wd_ref[...]))
    dgu_ref[:, :ff] = dgate
    dgu_ref[:, ff:] = dup
    hidden_t = hidden.T
    slots_into(send_ref, mine, cut[half:], hidden_t, y_ref)
    slots_into(keep0_ref, mine, cut[:half], hidden_t, y_ref)
    input_gradient(dx0_ref, dgate, dup, wg_ref, wu_ref)
    for copy in copies[5:]:
        copy.wait()
    slots_into(keep1_ref, mine, cut[:half], hidden1_ref[...].T, y1_ref)
    input_gradient(dx1_ref, dgu1_ref[:, :ff], dgu1_ref[:, ff:], wg1_ref, wu1_ref)


def rest(mine, inputs, cotangent, w_gate, w_up, w_down, dgu1, hidden1, cut, shard):
    _, _, rows, width = inputs.shape
    ff = w_gate.shape[3]
    half = len(cut) // 2
    outs = [(rows, 2 * ff)] + [(half, ff, shard)] * 3 + [(rows, width)] * 2
    held = (inputs, w_gate, w_up, cotangent, w_down, cotangent, w_gate, w_up)
    vmem = pl.BlockSpec(memory_space=pltpu.VMEM)
    return pl.pallas_call(
        functools.partial(rest_kernel, cut),
        out_shape=tuple(jax.ShapeDtypeStruct(dims, BF16) for dims in outs),
        in_specs=[pl.BlockSpec(memory_space=pltpu.SMEM)] + [pl.BlockSpec(memory_space=pl.ANY)] * 5 + [vmem] * 2,
        out_specs=[vmem] * len(outs),
        scratch_shapes=[pltpu.VMEM(array.shape[2:], BF16) for array in held] + [pltpu.SemaphoreType.DMA((8,))],
        compiler_params=pltpu.CompilerParams(vmem_limit_bytes=REST_LIMIT),
        cost_estimate=LONG,
        name="rest",
    )(mine, inputs, cotangent, w_gate, w_up, w_down, dgu1, hidden1)


def pair_kernel(mine, x0_ref, x1_ref, d0_ref, d1_ref, *outs):
    ff = outs[0].shape[1]
    x0, x1 = x0_ref[0, 0], x1_ref[0]
    for i, out in enumerate(outs):
        part = slice(i * ff, (i + 1) * ff)
        out[0] = (rows_dot(d0_ref[:, part], x0) + rows_dot(d1_ref[:, part], x1)).astype(BF16)


def pair(mine, inputs, mirrored_x, dgu, mirrored_dgu, offsets, shard, cost):
    _, _, rows, _ = inputs.shape
    both = dgu.shape[1]
    ff = both // 2
    count = len(offsets)

    def column(j, z):
        offset = sum(jnp.where(j == i, o, 0) for i, o in enumerate(offsets))
        return (0, 0, 0, z[0] ^ offset)

    return pl.pallas_call(
        pair_kernel,
        out_shape=(jax.ShapeDtypeStruct((count, ff, shard), BF16),) * 2,
        grid_spec=pltpu.PrefetchScalarGridSpec(
            num_scalar_prefetch=1,
            grid=(count,),
            in_specs=[
                pl.BlockSpec((1, 1, rows, shard), column),
                pl.BlockSpec((1, rows, shard), lambda j, z: (j, 0, 0)),
                pl.BlockSpec((rows, both), lambda j, z: (0, 0)),
                pl.BlockSpec((rows, both), lambda j, z: (0, 0)),
            ],
            out_specs=[pl.BlockSpec((1, ff, shard), lambda j, z: (j, 0, 0))] * 2,
        ),
        compiler_params=pltpu.CompilerParams(vmem_limit_bytes=VMEM_LIMIT),
        cost_estimate=cost,
        name="pair",
    )(mine, inputs, mirrored_x, dgu, mirrored_dgu)


def momentum_kernel(scale, count, *refs):
    moms, parts, outs = refs[:count], refs[count:-count], refs[-count:]
    ff = moms[0].shape[2]
    for i in range(count):
        total = parts[0][0, i * ff : (i + 1) * ff].astype(F32)
        for ref in parts[1:]:
            total = total + ref[0, i * ff : (i + 1) * ff].astype(F32)
        outs[i][0] = 0.9 * moms[i][0] + total.T * scale


def momentum(moms, parts, scale):
    shape = moms[0].shape
    _, shard, ff = shape
    count = len(moms)
    whole = pl.BlockSpec((1, shard, ff), lambda i: (0, 0, 0))
    return pl.pallas_call(
        functools.partial(momentum_kernel, scale, count),
        out_shape=(jax.ShapeDtypeStruct(shape, F32),) * count,
        grid=(1,),
        in_specs=[whole] * count + [pl.BlockSpec((1, ff * count, shard), lambda i: (0, 0, 0))] * len(parts),
        out_specs=[whole] * count,
        compiler_params=pltpu.CompilerParams(vmem_limit_bytes=2 * VMEM_LIMIT),
        cost_estimate=COST,
        name="momentum",
    )(*moms, *parts)


def shifted(value, steps, name):
    count = lax.axis_size("section")
    first, last = max(0, -steps), min(count, count - steps)
    with jax.named_scope(name):
        return lax.ppermute(value, "section", [(i, i + steps) for i in range(first, last)])


def mirrored(value, name):
    count = lax.axis_size("section")
    with jax.named_scope(name):
        return lax.ppermute(value, "section", [(i, count - 1 - i) for i in range(count)])


def swapped(value, mask, name):
    with jax.named_scope(name):
        return lax.ppermute(value, "dp", [(i, i ^ mask) for i in range(lax.axis_size("dp"))])


def after(value, earlier):
    return lax.optimization_barrier((value, earlier))[0]


def add(left, right):
    return (left.astype(F32) + right.astype(F32)).astype(BF16)


def halve(keep, received):
    (stay, go), (stayed, gone) = (jnp.split(v, 2, -3) for v in (keep, received))
    return add(stay, stayed), add(go, gone)


def join_kernel(first_ref, second_ref, out_ref):
    out_ref[0, 0] = first_ref[...]
    out_ref[0, 1] = second_ref[...]


def join(first, second):
    rows, width = first.shape
    step = min(64, rows)
    return pl.pallas_call(
        join_kernel,
        out_shape=jax.ShapeDtypeStruct((1, 2, rows, width), first.dtype),
        grid=(rows // step,),
        in_specs=[pl.BlockSpec((step, width), lambda i: (i, 0))] * 2,
        out_specs=pl.BlockSpec((1, 2, step, width), lambda i: (0, 0, i, 0)),
        compiler_params=pltpu.CompilerParams(vmem_limit_bytes=VMEM_LIMIT),
        cost_estimate=LONG,
        name="join",
    )(first, second)


def body(inputs, cotangent, w_gate, w_up, w_down, mom_gate, mom_up, mom_down):
    replicas = lax.axis_size("dp")
    _, _, rows, width = inputs.shape
    shard = width // replicas
    half = replicas // 2
    masks = [1 << i for i in range(replicas.bit_length() - 1)]
    cut = slot_offsets(replicas, masks)
    mine = lax.axis_index("dp")[None]
    scale = 1.0 / math.sqrt(rows * replicas)

    operands = (mine, inputs, cotangent, w_gate, w_up, w_down)

    dgu1, hidden1, send1, x_send, x_keep = second(*operands, cut, shard)
    dgu1_mirror = mirrored(dgu1, "dgu")
    x_send = mirrored(x_send, "x_send")
    first1 = swapped(send1, masks[0], "down1_first")
    x_keep = mirrored(x_keep, "x_keep")
    dgu0, send0, keep0, keep1, dx0, dx1 = rest(*operands, dgu1, hidden1, cut, shard)
    first0 = swapped(send0, masks[0], "down0_first")
    gate_send, up_send = pair(mine, inputs, x_send, dgu0, dgu1_mirror, cut[half:], shard, COST)
    gate = swapped(gate_send, masks[0], "gate_first")
    up = swapped(up_send, masks[0], "up_first")
    recv0 = shifted(after(dx0, gate_send), -1, "dx_first")
    recv1 = shifted(after(dx1, gate_send), 1, "dx_second")
    grad_in = join(recv0, recv1)
    gate_keep, up_keep = pair(mine, inputs, x_keep, dgu0, dgu1_mirror, cut[:half], shard, LONG)
    down_keep, down = jnp.stack([keep0, keep1]), jnp.stack([first0, first1])
    for mask in masks[1:]:
        down_keep, send = halve(down_keep, down)
        down = swapped(send, mask, "down_rest")
    for mask in masks[1:]:
        gate_keep, send = halve(gate_keep, gate)
        gate = swapped(send, mask, "gate_rest")
    for mask in masks[1:]:
        up_keep, send = halve(up_keep, up)
        up = swapped(after(send, down), mask, "up_rest")
    mirror = mirrored(add(down_keep[1], down[1]), "down_mirror")
    new_gate = momentum([mom_gate], (gate_keep, gate), scale)
    new_down = momentum([mom_down], (down_keep[0], down[0], mirror), scale)
    new_up = momentum([after(mom_up, (new_down, grad_in))], (up_keep, up), scale)
    return (grad_in, *new_gate, *new_up, *new_down)


def solution(mesh):
    tokens = P("section", None, "dp", None)
    weights = P("section", None, None, None)
    moments = P("section", "dp", None)
    return jax.shard_map(
        body,
        mesh=mesh,
        in_specs=(tokens, tokens, weights, weights, weights, moments, moments, moments),
        out_specs=(tokens, moments, moments, moments),
        check_vma=False,
    )
```

```python
import functools
import math

import jax
import jax.numpy as jnp
from jax import lax
from jax.experimental import pallas as pl
from jax.experimental.pallas import tpu as pltpu
from jax.sharding import PartitionSpec as P

BF16 = jnp.bfloat16
F32 = jnp.float32
VMEM_LIMIT = 8 * 1024 * 1024
SECOND_LIMIT = 58 * 1024 * 1024
REST_LIMIT = 54 * 1024 * 1024
COST = pl.CostEstimate(flops=1000, bytes_accessed=1000, transcendentals=0)
LONG = pl.CostEstimate(flops=1000, bytes_accessed=10**9, transcendentals=0)


def rows_dot(left, right):
    return lax.dot_general(left, right, (((0,), (0,)), ((), ())), preferred_element_type=F32)


def cols_dot(left, right):
    return lax.dot_general(left, right, (((1,), (1,)), ((), ())), preferred_element_type=F32)


def slot_offsets(count, masks):
    offsets = [0]
    for mask in reversed(masks):
        offsets = offsets + [o ^ mask for o in offsets]
    return offsets


def columns_of(mine, offset, shard):
    return pl.ds(pl.multiple_of((mine[0] ^ offset) * shard, shard), shard)


def reader(pairs, sems):
    copies = [pltpu.make_async_copy(source, target, sems.at[i]) for i, (source, target) in enumerate(pairs)]
    for copy in copies:
        copy.start()
    return copies


def backward(gate, up, dhid):
    sig = jax.nn.sigmoid(gate)
    act = gate * sig
    hidden = (act * up).astype(BF16)
    return hidden, (dhid * up * sig * (1.0 + gate * (1.0 - sig))).astype(BF16), (dhid * act).astype(BF16)


def slots_into(out_ref, mine, offsets, hidden_t, y_ref):
    shard = out_ref.shape[2]
    for slot, offset in enumerate(offsets):
        columns = y_ref[:, columns_of(mine, offset, shard)]
        out_ref[slot] = jnp.dot(hidden_t, columns, preferred_element_type=F32).astype(BF16)


def second_kernel(cut, far_cut, mine, x_hbm, y_hbm, wg_hbm, wu_hbm, wd_hbm, dgu_ref, hidden_ref, send_ref, message_ref, x_keep_ref, *held):
    (x_ref, wg_ref, wu_ref, y_ref, wd_ref), sems, slot_sems = held[:5], held[5], held[6]
    half, ff, shard = send_ref.shape
    hbm = (x_hbm, wg_hbm, wu_hbm, y_hbm, wd_hbm)
    copies = reader([(source.at[0, 1], target) for source, target in zip(hbm, held)], sems)
    copies[0].wait()
    slots = reader(
        [
            (x_ref.at[:, columns_of(mine, offset, shard)], (x_keep_ref if i < half else message_ref).at[i % half])
            for i, offset in enumerate(cut)
        ],
        slot_sems,
    )
    copies[1].wait()
    gate = jnp.dot(x_ref[...], wg_ref[...], preferred_element_type=F32)
    copies[2].wait()
    up = jnp.dot(x_ref[...], wu_ref[...], preferred_element_type=F32)
    copies[3].wait()
    copies[4].wait()
    dhid = cols_dot(y_ref[...], wd_ref[...])
    hidden, dgate, dup = backward(gate, up, dhid)
    dgu_ref[:, :ff] = dgate
    dgu_ref[:, ff:] = dup
    for i in range(half, message_ref.shape[0]):
        message_ref[i] = dgu_ref[:, (i - half) * shard : (i - half + 1) * shard]
    hidden_ref[...] = hidden
    slots_into(send_ref, mine, far_cut[half:], hidden.T, y_ref)
    for copy in slots:
        copy.wait()


def second(mine, inputs, cotangent, w_gate, w_up, w_down, cut, far_cut, shard):
    _, _, rows, width = inputs.shape
    ff = w_gate.shape[3]
    half = len(cut) // 2
    outs = [(rows, 2 * ff), (rows, ff), (half, ff, shard), (half + 2 * ff // shard, rows, shard), (half, rows, shard)]
    return pl.pallas_call(
        functools.partial(second_kernel, cut, far_cut),
        out_shape=tuple(jax.ShapeDtypeStruct(dims, BF16) for dims in outs),
        in_specs=[pl.BlockSpec(memory_space=pltpu.SMEM)] + [pl.BlockSpec(memory_space=pl.ANY)] * 5,
        out_specs=[pl.BlockSpec(memory_space=pltpu.VMEM)] * len(outs),
        scratch_shapes=[pltpu.VMEM(array.shape[2:], BF16) for array in (inputs, w_gate, w_up, cotangent, w_down)]
        + [pltpu.SemaphoreType.DMA((5,)), pltpu.SemaphoreType.DMA((len(cut),))],
        compiler_params=pltpu.CompilerParams(vmem_limit_bytes=SECOND_LIMIT),
        cost_estimate=LONG,
        name="second",
    )(mine, inputs, cotangent, w_gate, w_up, w_down)


def rest_kernel(cut, far_cut, mine, x_hbm, y_hbm, wg_hbm, wu_hbm, wd_hbm, dgu1_ref, hidden1_ref, *refs):
    dgu_ref, send_ref, keep0_ref, keep1_ref, dx0_ref, dx1_ref = refs[:6]
    (x_ref, wg_ref, wu_ref, y_ref, wd_ref, y1_ref, wg1_ref, wu1_ref), sems = refs[6:14], refs[14]
    half, ff, shard = send_ref.shape
    width = x_ref.shape[1]
    hbm = (x_hbm, wg_hbm, wu_hbm, y_hbm, wd_hbm)
    sources = [source.at[0, 0] for source in hbm] + [source.at[0, 1] for source in (y_hbm, wg_hbm, wu_hbm)]
    copies = reader(list(zip(sources, refs[6:14])), sems)

    def input_gradient(out_ref, dgate, dup, wg, wu):
        step = min(512, width)
        for start in range(0, width, step):
            rows = pl.ds(start, step)
            out_ref[:, rows] = (cols_dot(dgate, wg[rows, :]) + cols_dot(dup, wu[rows, :])).astype(BF16)

    copies[0].wait()
    copies[1].wait()
    gate = jnp.dot(x_ref[...], wg_ref[...], preferred_element_type=F32)
    copies[2].wait()
    up = jnp.dot(x_ref[...], wu_ref[...], preferred_element_type=F32)
    copies[3].wait()
    copies[4].wait()
    hidden, dgate, dup = backward(gate, up, cols_dot(y_ref[...], wd_ref[...]))
    dgu_ref[:, :ff] = dgate
    dgu_ref[:, ff:] = dup
    hidden_t = hidden.T
    slots_into(send_ref, mine, cut[half:], hidden_t, y_ref)
    slots_into(keep0_ref, mine, cut[:half], hidden_t, y_ref)
    input_gradient(dx0_ref, dgate, dup, wg_ref, wu_ref)
    for copy in copies[5:]:
        copy.wait()
    slots_into(keep1_ref, mine, far_cut[:half], hidden1_ref[...].T, y1_ref)
    input_gradient(dx1_ref, dgu1_ref[:, :ff], dgu1_ref[:, ff:], wg1_ref, wu1_ref)


def rest(mine, inputs, cotangent, w_gate, w_up, w_down, dgu1, hidden1, cut, far_cut, shard):
    _, _, rows, width = inputs.shape
    ff = w_gate.shape[3]
    half = len(cut) // 2
    outs = [(rows, 2 * ff)] + [(half, ff, shard)] * 3 + [(rows, width)] * 2
    held = (inputs, w_gate, w_up, cotangent, w_down, cotangent, w_gate, w_up)
    vmem = pl.BlockSpec(memory_space=pltpu.VMEM)
    return pl.pallas_call(
        functools.partial(rest_kernel, cut, far_cut),
        out_shape=tuple(jax.ShapeDtypeStruct(dims, BF16) for dims in outs),
        in_specs=[pl.BlockSpec(memory_space=pltpu.SMEM)] + [pl.BlockSpec(memory_space=pl.ANY)] * 5 + [vmem] * 2,
        out_specs=[vmem] * len(outs),
        scratch_shapes=[pltpu.VMEM(array.shape[2:], BF16) for array in held] + [pltpu.SemaphoreType.DMA((8,))],
        compiler_params=pltpu.CompilerParams(vmem_limit_bytes=REST_LIMIT),
        cost_estimate=LONG,
        name="rest",
    )(mine, inputs, cotangent, w_gate, w_up, w_down, dgu1, hidden1)


def pair_kernel(mine, x0_ref, x1_ref, d0_ref, d1_ref, *outs):
    ff = outs[0].shape[1]
    x0, x1 = x0_ref[0, 0], x1_ref[0]
    d1 = jnp.concatenate([d1_ref[i] for i in range(d1_ref.shape[0])], axis=1)
    for i, out in enumerate(outs):
        part = slice(i * ff, (i + 1) * ff)
        out[0] = (rows_dot(d0_ref[:, part], x0) + rows_dot(d1[:, part], x1)).astype(BF16)


def pair(mine, inputs, mirrored_x, dgu, message, offsets, shard):
    _, _, rows, _ = inputs.shape
    both = dgu.shape[1]
    ff = both // 2
    count = len(offsets)

    def column(j, z):
        offset = sum(jnp.where(j == i, o, 0) for i, o in enumerate(offsets))
        return (0, 0, 0, z[0] ^ offset)

    pieces = both // shard
    return pl.pallas_call(
        pair_kernel,
        out_shape=(jax.ShapeDtypeStruct((count, ff, shard), BF16),) * 2,
        grid_spec=pltpu.PrefetchScalarGridSpec(
            num_scalar_prefetch=1,
            grid=(count,),
            in_specs=[
                pl.BlockSpec((1, 1, rows, shard), column),
                pl.BlockSpec((1, rows, shard), lambda j, z: (j, 0, 0)),
                pl.BlockSpec((rows, both), lambda j, z: (0, 0)),
                pl.BlockSpec((pieces, rows, shard), lambda j, z: (count // pieces, 0, 0)),
            ],
            out_specs=[pl.BlockSpec((1, ff, shard), lambda j, z: (j, 0, 0))] * 2,
        ),
        compiler_params=pltpu.CompilerParams(vmem_limit_bytes=VMEM_LIMIT),
        cost_estimate=LONG,
        name="pair",
    )(mine, inputs, mirrored_x, dgu, message)


def momentum_kernel(scale, count, *refs):
    moms, parts, outs = refs[:count], refs[count:-count], refs[-count:]
    ff = moms[0].shape[2]
    for i in range(count):
        total = parts[0][0, i * ff : (i + 1) * ff].astype(F32)
        for ref in parts[1:]:
            total = total + ref[0, i * ff : (i + 1) * ff].astype(F32)
        outs[i][0] = 0.9 * moms[i][0] + total.T * scale


def momentum(moms, parts, scale):
    shape = moms[0].shape
    _, shard, ff = shape
    count = len(moms)
    whole = pl.BlockSpec((1, shard, ff), lambda i: (0, 0, 0))
    return pl.pallas_call(
        functools.partial(momentum_kernel, scale, count),
        out_shape=(jax.ShapeDtypeStruct(shape, F32),) * count,
        grid=(1,),
        in_specs=[whole] * count + [pl.BlockSpec((1, ff * count, shard), lambda i: (0, 0, 0))] * len(parts),
        out_specs=[whole] * count,
        compiler_params=pltpu.CompilerParams(vmem_limit_bytes=2 * VMEM_LIMIT),
        cost_estimate=COST,
        name="momentum",
    )(*moms, *parts)


def shifted(value, steps, name):
    count = lax.axis_size("section")
    first, last = max(0, -steps), min(count, count - steps)
    with jax.named_scope(name):
        return lax.ppermute(value, "section", [(i, i + steps) for i in range(first, last)])


def mirrored(value, name):
    count = lax.axis_size("section")
    with jax.named_scope(name):
        return lax.ppermute(value, "section", [(i, count - 1 - i) for i in range(count)])


def swapped(value, mask, name):
    with jax.named_scope(name):
        return lax.ppermute(value, "dp", [(i, i ^ mask) for i in range(lax.axis_size("dp"))])


def after(value, earlier):
    return lax.optimization_barrier((value, earlier))[0]


def add(left, right):
    return (left.astype(F32) + right.astype(F32)).astype(BF16)


def halve(keep, received):
    (stay, go), (stayed, gone) = (jnp.split(v, 2, -3) for v in (keep, received))
    return add(stay, stayed), add(go, gone)


def join_kernel(first_ref, second_ref, out_ref):
    out_ref[0, 0] = first_ref[...]
    out_ref[0, 1] = second_ref[...]


def join(first, second):
    rows, width = first.shape
    step = min(64, rows)
    return pl.pallas_call(
        join_kernel,
        out_shape=jax.ShapeDtypeStruct((1, 2, rows, width), first.dtype),
        grid=(rows // step,),
        in_specs=[pl.BlockSpec((step, width), lambda i: (i, 0))] * 2,
        out_specs=pl.BlockSpec((1, 2, step, width), lambda i: (0, 0, i, 0)),
        compiler_params=pltpu.CompilerParams(vmem_limit_bytes=VMEM_LIMIT),
        cost_estimate=LONG,
        name="join",
    )(first, second)


def body(inputs, cotangent, w_gate, w_up, w_down, mom_gate, mom_up, mom_down):
    replicas = lax.axis_size("dp")
    _, _, rows, width = inputs.shape
    shard = width // replicas
    half = replicas // 2
    masks = [1 << i for i in range(replicas.bit_length() - 1)]
    cut = slot_offsets(replicas, masks)
    mine = lax.axis_index("dp")[None]
    scale = 1.0 / math.sqrt(rows * replicas)

    operands = (mine, inputs, cotangent, w_gate, w_up, w_down)

    dgu1, hidden1, send1, message, x_keep = second(*operands, cut, cut, shard)
    message = mirrored(message, "message")
    first1 = swapped(send1, masks[0], "down1_first")
    x_keep = mirrored(x_keep, "x_keep")
    dgu0, send0, keep0, keep1, dx0, dx1 = rest(*operands, dgu1, hidden1, cut, cut, shard)
    first0 = swapped(send0, masks[0], "down0_first")
    for mask in masks[1:]:
        keep1, send1 = halve(keep1, first1)
        first1 = swapped(send1, mask, "down1_rest")
    gate_send, up_send = pair(mine, inputs, message, after(dgu0, send1), message, cut[half:], shard)
    gate = swapped(gate_send, masks[0], "gate_first")
    up = swapped(up_send, masks[0], "up_first")
    gate_first = gate
    recv0 = shifted(after(dx0, gate_send), -1, "dx_first")
    recv1 = shifted(after(dx1, gate_send), 1, "dx_second")
    grad_in = join(recv0, recv1)
    gate_keep, up_keep = pair(mine, inputs, x_keep, dgu0, message, cut[:half], shard)
    for mask in masks[1:]:
        keep0, send = halve(keep0, first0)
        first0 = swapped(send, mask, "down0_rest")
    for mask in masks[1:]:
        gate_keep, send = halve(gate_keep, gate)
        gate = swapped(after(send, first0), mask, "gate_rest")
    for mask in masks[1:]:
        up_keep, send = halve(up_keep, up)
        up = swapped(send, mask, "up_rest")
    mirror = mirrored(after(add(keep1, first1), gate_first), "down_mirror")
    new_up = momentum([mom_up], (up_keep, up), scale)
    new_down = momentum([mom_down], (keep0, first0, mirror), scale)
    new_gate = momentum([after(mom_gate, (new_down, grad_in))], (gate_keep, gate), scale)
    return (grad_in, *new_gate, *new_up, *new_down)


def solution(mesh):
    tokens = P("section", None, "dp", None)
    weights = P("section", None, None, None)
    moments = P("section", "dp", None)
    return jax.shard_map(
        body,
        mesh=mesh,
        in_specs=(tokens, tokens, weights, weights, weights, moments, moments, moments),
        out_specs=(tokens, moments, moments, moments),
        check_vma=False,
    )
```

```python
import functools
import math

import jax
import jax.numpy as jnp
from jax import lax
from jax.experimental import pallas as pl
from jax.experimental.pallas import tpu as pltpu
from jax.sharding import PartitionSpec as P

BF16 = jnp.bfloat16
F32 = jnp.float32
VMEM_LIMIT = 8 * 1024 * 1024
SECOND_LIMIT = 58 * 1024 * 1024
REST_LIMIT = 54 * 1024 * 1024
COST = pl.CostEstimate(flops=1000, bytes_accessed=1000, transcendentals=0)
LONG = pl.CostEstimate(flops=1000, bytes_accessed=10**9, transcendentals=0)


def rows_dot(left, right):
    return lax.dot_general(left, right, (((0,), (0,)), ((), ())), preferred_element_type=F32)


def cols_dot(left, right):
    return lax.dot_general(left, right, (((1,), (1,)), ((), ())), preferred_element_type=F32)


def slot_offsets(count, masks):
    offsets = [0]
    for mask in reversed(masks):
        offsets = offsets + [o ^ mask for o in offsets]
    return offsets


def columns_of(mine, offset, shard):
    return pl.ds(pl.multiple_of((mine[0] ^ offset) * shard, shard), shard)


def reader(pairs, sems):
    copies = [pltpu.make_async_copy(source, target, sems.at[i]) for i, (source, target) in enumerate(pairs)]
    for copy in copies:
        copy.start()
    return copies


def backward(gate, up, dhid):
    sig = jax.nn.sigmoid(gate)
    act = gate * sig
    hidden = (act * up).astype(BF16)
    return hidden, (dhid * up * sig * (1.0 + gate * (1.0 - sig))).astype(BF16), (dhid * act).astype(BF16)


def slots_into(out_ref, mine, offsets, hidden_t, y_ref):
    shard = out_ref.shape[2]
    for slot, offset in enumerate(offsets):
        columns = y_ref[:, columns_of(mine, offset, shard)]
        out_ref[slot] = jnp.dot(hidden_t, columns, preferred_element_type=F32).astype(BF16)


def second_kernel(cut, far_cut, mine, x_hbm, y_hbm, wg_hbm, wu_hbm, wd_hbm, dgu_ref, hidden_ref, send_ref, message_ref, x_keep_ref, *held):
    (x_ref, wg_ref, wu_ref, y_ref, wd_ref), sems, slot_sems = held[:5], held[5], held[6]
    half, ff, shard = send_ref.shape
    hbm = (x_hbm, wg_hbm, wu_hbm, y_hbm, wd_hbm)
    copies = reader([(source.at[0, 1], target) for source, target in zip(hbm, held)], sems)
    copies[0].wait()
    slots = reader(
        [
            (x_ref.at[:, columns_of(mine, offset, shard)], (x_keep_ref if i < half else message_ref).at[i % half])
            for i, offset in enumerate(cut)
        ],
        slot_sems,
    )
    copies[1].wait()
    gate = jnp.dot(x_ref[...], wg_ref[...], preferred_element_type=F32)
    copies[2].wait()
    up = jnp.dot(x_ref[...], wu_ref[...], preferred_element_type=F32)
    copies[3].wait()
    copies[4].wait()
    dhid = cols_dot(y_ref[...], wd_ref[...])
    hidden, dgate, dup = backward(gate, up, dhid)
    dgu_ref[:, :ff] = dgate
    dgu_ref[:, ff:] = dup
    for i in range(half, message_ref.shape[0]):
        message_ref[i] = dgu_ref[:, (i - half) * shard : (i - half + 1) * shard]
    hidden_ref[...] = hidden
    slots_into(send_ref, mine, far_cut[half:], hidden.T, y_ref)
    for copy in slots:
        copy.wait()


def second(mine, inputs, cotangent, w_gate, w_up, w_down, cut, far_cut, shard):
    _, _, rows, width = inputs.shape
    ff = w_gate.shape[3]
    half = len(cut) // 2
    outs = [(rows, 2 * ff), (rows, ff), (half, ff, shard), (half + 2 * ff // shard, rows, shard), (half, rows, shard)]
    return pl.pallas_call(
        functools.partial(second_kernel, cut, far_cut),
        out_shape=tuple(jax.ShapeDtypeStruct(dims, BF16) for dims in outs),
        in_specs=[pl.BlockSpec(memory_space=pltpu.SMEM)] + [pl.BlockSpec(memory_space=pl.ANY)] * 5,
        out_specs=[pl.BlockSpec(memory_space=pltpu.VMEM)] * len(outs),
        scratch_shapes=[pltpu.VMEM(array.shape[2:], BF16) for array in (inputs, w_gate, w_up, cotangent, w_down)]
        + [pltpu.SemaphoreType.DMA((5,)), pltpu.SemaphoreType.DMA((len(cut),))],
        compiler_params=pltpu.CompilerParams(vmem_limit_bytes=SECOND_LIMIT),
        cost_estimate=LONG,
        name="second",
    )(mine, inputs, cotangent, w_gate, w_up, w_down)


def rest_kernel(cut, far_cut, mine, x_hbm, y_hbm, wg_hbm, wu_hbm, wd_hbm, dgu1_ref, hidden1_ref, *refs):
    dgu_ref, send_ref, keep0_ref, keep1_ref, dx0_ref, dx1_ref = refs[:6]
    (x_ref, wg_ref, wu_ref, y_ref, wd_ref, y1_ref, wg1_ref, wu1_ref), sems = refs[6:14], refs[14]
    half, ff, shard = send_ref.shape
    width = x_ref.shape[1]
    hbm = (x_hbm, wg_hbm, wu_hbm, y_hbm, wd_hbm)
    sources = [source.at[0, 0] for source in hbm] + [source.at[0, 1] for source in (y_hbm, wg_hbm, wu_hbm)]
    copies = reader(list(zip(sources, refs[6:14])), sems)

    def input_gradient(out_ref, dgate, dup, wg, wu):
        step = min(512, width)
        for start in range(0, width, step):
            rows = pl.ds(start, step)
            out_ref[:, rows] = (cols_dot(dgate, wg[rows, :]) + cols_dot(dup, wu[rows, :])).astype(BF16)

    copies[0].wait()
    copies[1].wait()
    gate = jnp.dot(x_ref[...], wg_ref[...], preferred_element_type=F32)
    copies[2].wait()
    up = jnp.dot(x_ref[...], wu_ref[...], preferred_element_type=F32)
    copies[3].wait()
    copies[4].wait()
    hidden, dgate, dup = backward(gate, up, cols_dot(y_ref[...], wd_ref[...]))
    dgu_ref[:, :ff] = dgate
    dgu_ref[:, ff:] = dup
    hidden_t = hidden.T
    slots_into(send_ref, mine, cut[half:], hidden_t, y_ref)
    slots_into(keep0_ref, mine, cut[:half], hidden_t, y_ref)
    input_gradient(dx0_ref, dgate, dup, wg_ref, wu_ref)
    for copy in copies[5:]:
        copy.wait()
    slots_into(keep1_ref, mine, far_cut[:half], hidden1_ref[...].T, y1_ref)
    input_gradient(dx1_ref, dgu1_ref[:, :ff], dgu1_ref[:, ff:], wg1_ref, wu1_ref)


def rest(mine, inputs, cotangent, w_gate, w_up, w_down, dgu1, hidden1, cut, far_cut, shard):
    _, _, rows, width = inputs.shape
    ff = w_gate.shape[3]
    half = len(cut) // 2
    outs = [(rows, 2 * ff)] + [(half, ff, shard)] * 3 + [(rows, width)] * 2
    held = (inputs, w_gate, w_up, cotangent, w_down, cotangent, w_gate, w_up)
    vmem = pl.BlockSpec(memory_space=pltpu.VMEM)
    return pl.pallas_call(
        functools.partial(rest_kernel, cut, far_cut),
        out_shape=tuple(jax.ShapeDtypeStruct(dims, BF16) for dims in outs),
        in_specs=[pl.BlockSpec(memory_space=pltpu.SMEM)] + [pl.BlockSpec(memory_space=pl.ANY)] * 5 + [vmem] * 2,
        out_specs=[vmem] * len(outs),
        scratch_shapes=[pltpu.VMEM(array.shape[2:], BF16) for array in held] + [pltpu.SemaphoreType.DMA((8,))],
        compiler_params=pltpu.CompilerParams(vmem_limit_bytes=REST_LIMIT),
        cost_estimate=LONG,
        name="rest",
    )(mine, inputs, cotangent, w_gate, w_up, w_down, dgu1, hidden1)


def pair_kernel(mine, x0_ref, x1_ref, d0_ref, d1_ref, *outs):
    ff = outs[0].shape[1]
    x0, x1 = x0_ref[0, 0], x1_ref[0]
    d1 = jnp.concatenate([d1_ref[i] for i in range(d1_ref.shape[0])], axis=1)
    for i, out in enumerate(outs):
        part = slice(i * ff, (i + 1) * ff)
        out[0] = (rows_dot(d0_ref[:, part], x0) + rows_dot(d1[:, part], x1)).astype(BF16)


def pair(mine, inputs, mirrored_x, dgu, message, offsets, shard):
    _, _, rows, _ = inputs.shape
    both = dgu.shape[1]
    ff = both // 2
    count = len(offsets)

    def column(j, z):
        offset = sum(jnp.where(j == i, o, 0) for i, o in enumerate(offsets))
        return (0, 0, 0, z[0] ^ offset)

    pieces = both // shard
    return pl.pallas_call(
        pair_kernel,
        out_shape=(jax.ShapeDtypeStruct((count, ff, shard), BF16),) * 2,
        grid_spec=pltpu.PrefetchScalarGridSpec(
            num_scalar_prefetch=1,
            grid=(count,),
            in_specs=[
                pl.BlockSpec((1, 1, rows, shard), column),
                pl.BlockSpec((1, rows, shard), lambda j, z: (j, 0, 0)),
                pl.BlockSpec((rows, both), lambda j, z: (0, 0)),
                pl.BlockSpec((pieces, rows, shard), lambda j, z: (count // pieces, 0, 0)),
            ],
            out_specs=[pl.BlockSpec((1, ff, shard), lambda j, z: (j, 0, 0))] * 2,
        ),
        compiler_params=pltpu.CompilerParams(vmem_limit_bytes=VMEM_LIMIT),
        cost_estimate=LONG,
        name="pair",
    )(mine, inputs, mirrored_x, dgu, message)


def momentum_kernel(scale, count, *refs):
    moms, parts, outs = refs[:count], refs[count:-count], refs[-count:]
    ff = moms[0].shape[2]
    for i in range(count):
        total = parts[0][0, i * ff : (i + 1) * ff].astype(F32)
        for ref in parts[1:]:
            total = total + ref[0, i * ff : (i + 1) * ff].astype(F32)
        outs[i][0] = 0.9 * moms[i][0] + total.T * scale


def momentum(moms, parts, scale):
    shape = moms[0].shape
    _, shard, ff = shape
    count = len(moms)
    whole = pl.BlockSpec((1, shard, ff), lambda i: (0, 0, 0))
    return pl.pallas_call(
        functools.partial(momentum_kernel, scale, count),
        out_shape=(jax.ShapeDtypeStruct(shape, F32),) * count,
        grid=(1,),
        in_specs=[whole] * count + [pl.BlockSpec((1, ff * count, shard), lambda i: (0, 0, 0))] * len(parts),
        out_specs=[whole] * count,
        compiler_params=pltpu.CompilerParams(vmem_limit_bytes=2 * VMEM_LIMIT),
        cost_estimate=COST,
        name="momentum",
    )(*moms, *parts)


def shifted(value, steps, name):
    count = lax.axis_size("section")
    first, last = max(0, -steps), min(count, count - steps)
    with jax.named_scope(name):
        return lax.ppermute(value, "section", [(i, i + steps) for i in range(first, last)])


def mirrored(value, name):
    count = lax.axis_size("section")
    with jax.named_scope(name):
        return lax.ppermute(value, "section", [(i, count - 1 - i) for i in range(count)])


def swapped(value, mask, name):
    with jax.named_scope(name):
        return lax.ppermute(value, "dp", [(i, i ^ mask) for i in range(lax.axis_size("dp"))])


def after(value, earlier):
    return lax.optimization_barrier((value, earlier))[0]


def add(left, right):
    return (left.astype(F32) + right.astype(F32)).astype(BF16)


def halve(keep, received):
    (stay, go), (stayed, gone) = (jnp.split(v, 2, -3) for v in (keep, received))
    return add(stay, stayed), add(go, gone)


def join_kernel(first_ref, second_ref, out_ref):
    out_ref[0, 0] = first_ref[...]
    out_ref[0, 1] = second_ref[...]


def join(first, second):
    rows, width = first.shape
    step = min(64, rows)
    return pl.pallas_call(
        join_kernel,
        out_shape=jax.ShapeDtypeStruct((1, 2, rows, width), first.dtype),
        grid=(rows // step,),
        in_specs=[pl.BlockSpec((step, width), lambda i: (i, 0))] * 2,
        out_specs=pl.BlockSpec((1, 2, step, width), lambda i: (0, 0, i, 0)),
        compiler_params=pltpu.CompilerParams(vmem_limit_bytes=VMEM_LIMIT),
        cost_estimate=LONG,
        name="join",
    )(first, second)


def body(inputs, cotangent, w_gate, w_up, w_down, mom_gate, mom_up, mom_down):
    replicas = lax.axis_size("dp")
    _, _, rows, width = inputs.shape
    shard = width // replicas
    half = replicas // 2
    masks = [1 << i for i in range(replicas.bit_length() - 1)]
    cut = slot_offsets(replicas, masks)
    mine = lax.axis_index("dp")[None]
    scale = 1.0 / math.sqrt(rows * replicas)

    operands = (mine, inputs, cotangent, w_gate, w_up, w_down)

    dgu1, hidden1, send1, message, x_keep = second(*operands, cut, cut, shard)
    message = mirrored(message, "message")
    first1 = swapped(send1, masks[0], "down1_first")
    x_keep = mirrored(after(x_keep, message), "x_keep")
    dgu0, send0, keep0, keep1, dx0, dx1 = rest(*operands, dgu1, hidden1, cut, cut, shard)
    first0 = swapped(send0, masks[0], "down0_first")
    for mask in masks[1:]:
        keep1, send1 = halve(keep1, first1)
        first1 = swapped(send1, mask, "down1_rest")
    gate_send, up_send = pair(mine, inputs, message, after(dgu0, send1), message, cut[half:], shard)
    gate = swapped(gate_send, masks[0], "gate_first")
    up = swapped(up_send, masks[0], "up_first")
    gate_first = gate
    recv0 = shifted(after(dx0, gate_send), -1, "dx_first")
    recv1 = shifted(after(dx1, gate_send), 1, "dx_second")
    grad_in = join(recv0, recv1)
    gate_keep, up_keep = pair(mine, inputs, x_keep, dgu0, message, cut[:half], shard)
    for mask in masks[1:]:
        keep0, send = halve(keep0, first0)
        first0 = swapped(send, mask, "down0_rest")
    for mask in masks[1:]:
        gate_keep, send = halve(gate_keep, gate)
        gate = swapped(after(send, first0), mask, "gate_rest")
    for mask in masks[1:]:
        up_keep, send = halve(up_keep, up)
        up = swapped(send, mask, "up_rest")
    mirror = mirrored(after(add(keep1, first1), gate_first), "down_mirror")
    new_up = momentum([mom_up], (up_keep, up), scale)
    new_down = momentum([mom_down], (keep0, first0, mirror), scale)
    new_gate = momentum([after(mom_gate, (new_down, grad_in))], (gate_keep, gate), scale)
    return (grad_in, *new_gate, *new_up, *new_down)


def solution(mesh):
    tokens = P("section", None, "dp", None)
    weights = P("section", None, None, None)
    moments = P("section", "dp", None)
    return jax.shard_map(
        body,
        mesh=mesh,
        in_specs=(tokens, tokens, weights, weights, weights, moments, moments, moments),
        out_specs=(tokens, moments, moments, moments),
        check_vma=False,
    )
```

```python
import functools
import math

import jax
import jax.numpy as jnp
from jax import lax
from jax.experimental import pallas as pl
from jax.experimental.pallas import tpu as pltpu
from jax.sharding import PartitionSpec as P

BF16 = jnp.bfloat16
F32 = jnp.float32
VMEM_LIMIT = 8 * 1024 * 1024
SECOND_LIMIT = 58 * 1024 * 1024
REST_LIMIT = 54 * 1024 * 1024
COST = pl.CostEstimate(flops=1000, bytes_accessed=1000, transcendentals=0)
LONG = pl.CostEstimate(flops=1000, bytes_accessed=10**9, transcendentals=0)


def rows_dot(left, right):
    return lax.dot_general(left, right, (((0,), (0,)), ((), ())), preferred_element_type=F32)


def cols_dot(left, right):
    return lax.dot_general(left, right, (((1,), (1,)), ((), ())), preferred_element_type=F32)


def slot_offsets(count, masks):
    offsets = [0]
    for mask in reversed(masks):
        offsets = offsets + [o ^ mask for o in offsets]
    return offsets


def columns_of(mine, offset, shard):
    return pl.ds(pl.multiple_of((mine[0] ^ offset) * shard, shard), shard)


def reader(pairs, sems):
    copies = [pltpu.make_async_copy(source, target, sems.at[i]) for i, (source, target) in enumerate(pairs)]
    for copy in copies:
        copy.start()
    return copies


def backward(gate, up, dhid):
    sig = jax.nn.sigmoid(gate)
    act = gate * sig
    hidden = (act * up).astype(BF16)
    return hidden, (dhid * up * sig * (1.0 + gate * (1.0 - sig))).astype(BF16), (dhid * act).astype(BF16)


def slots_into(out_ref, mine, offsets, hidden_t, y_ref):
    shard = out_ref.shape[2]
    for slot, offset in enumerate(offsets):
        columns = y_ref[:, columns_of(mine, offset, shard)]
        out_ref[slot] = jnp.dot(hidden_t, columns, preferred_element_type=F32).astype(BF16)


def second_kernel(cut, far_cut, mine, x_hbm, y_hbm, wg_hbm, wu_hbm, wd_hbm, dgu_ref, hidden_ref, send_ref, message_ref, x_keep_ref, *held):
    (x_ref, wg_ref, wu_ref, y_ref, wd_ref), sems, slot_sems = held[:5], held[5], held[6]
    half, ff, shard = send_ref.shape
    hbm = (x_hbm, wg_hbm, wu_hbm, y_hbm, wd_hbm)
    copies = reader([(source.at[0, 1], target) for source, target in zip(hbm, held)], sems)
    copies[0].wait()
    slots = reader(
        [
            (x_ref.at[:, columns_of(mine, offset, shard)], (x_keep_ref if i < half else message_ref).at[i % half])
            for i, offset in enumerate(cut)
        ],
        slot_sems,
    )
    copies[1].wait()
    gate = jnp.dot(x_ref[...], wg_ref[...], preferred_element_type=F32)
    copies[2].wait()
    up = jnp.dot(x_ref[...], wu_ref[...], preferred_element_type=F32)
    copies[3].wait()
    copies[4].wait()
    dhid = cols_dot(y_ref[...], wd_ref[...])
    hidden, dgate, dup = backward(gate, up, dhid)
    dgu_ref[:, :ff] = dgate
    dgu_ref[:, ff:] = dup
    for i in range(half, message_ref.shape[0]):
        message_ref[i] = dgu_ref[:, (i - half) * shard : (i - half + 1) * shard]
    hidden_ref[...] = hidden
    slots_into(send_ref, mine, far_cut[half:], hidden.T, y_ref)
    for copy in slots:
        copy.wait()


def second(mine, inputs, cotangent, w_gate, w_up, w_down, cut, far_cut, shard):
    _, _, rows, width = inputs.shape
    ff = w_gate.shape[3]
    half = len(cut) // 2
    outs = [(rows, 2 * ff), (rows, ff), (half, ff, shard), (half + 2 * ff // shard, rows, shard), (half, rows, shard)]
    return pl.pallas_call(
        functools.partial(second_kernel, cut, far_cut),
        out_shape=tuple(jax.ShapeDtypeStruct(dims, BF16) for dims in outs),
        in_specs=[pl.BlockSpec(memory_space=pltpu.SMEM)] + [pl.BlockSpec(memory_space=pl.ANY)] * 5,
        out_specs=[pl.BlockSpec(memory_space=pltpu.VMEM)] * len(outs),
        scratch_shapes=[pltpu.VMEM(array.shape[2:], BF16) for array in (inputs, w_gate, w_up, cotangent, w_down)]
        + [pltpu.SemaphoreType.DMA((5,)), pltpu.SemaphoreType.DMA((len(cut),))],
        compiler_params=pltpu.CompilerParams(vmem_limit_bytes=SECOND_LIMIT),
        cost_estimate=LONG,
        name="second",
    )(mine, inputs, cotangent, w_gate, w_up, w_down)


def rest_kernel(cut, far_cut, mine, x_hbm, y_hbm, wg_hbm, wu_hbm, wd_hbm, dgu1_ref, hidden1_ref, *refs):
    dgu_ref, send_ref, keep0_ref, keep1_ref, dx0_ref, dx1_ref = refs[:6]
    (x_ref, wg_ref, wu_ref, y_ref, wd_ref, y1_ref, wg1_ref, wu1_ref), sems = refs[6:14], refs[14]
    half, ff, shard = send_ref.shape
    width = x_ref.shape[1]
    hbm = (x_hbm, wg_hbm, wu_hbm, y_hbm, wd_hbm)
    sources = [source.at[0, 0] for source in hbm] + [source.at[0, 1] for source in (y_hbm, wg_hbm, wu_hbm)]
    copies = reader(list(zip(sources, refs[6:14])), sems)

    def input_gradient(out_ref, dgate, dup, wg, wu):
        step = min(512, width)
        for start in range(0, width, step):
            rows = pl.ds(start, step)
            out_ref[:, rows] = (cols_dot(dgate, wg[rows, :]) + cols_dot(dup, wu[rows, :])).astype(BF16)

    copies[0].wait()
    copies[1].wait()
    gate = jnp.dot(x_ref[...], wg_ref[...], preferred_element_type=F32)
    copies[2].wait()
    up = jnp.dot(x_ref[...], wu_ref[...], preferred_element_type=F32)
    copies[3].wait()
    copies[4].wait()
    hidden, dgate, dup = backward(gate, up, cols_dot(y_ref[...], wd_ref[...]))
    dgu_ref[:, :ff] = dgate
    dgu_ref[:, ff:] = dup
    hidden_t = hidden.T
    slots_into(send_ref, mine, cut[half:], hidden_t, y_ref)
    slots_into(keep0_ref, mine, cut[:half], hidden_t, y_ref)
    input_gradient(dx0_ref, dgate, dup, wg_ref, wu_ref)
    for copy in copies[5:]:
        copy.wait()
    slots_into(keep1_ref, mine, far_cut[:half], hidden1_ref[...].T, y1_ref)
    input_gradient(dx1_ref, dgu1_ref[:, :ff], dgu1_ref[:, ff:], wg1_ref, wu1_ref)


def rest(mine, inputs, cotangent, w_gate, w_up, w_down, dgu1, hidden1, cut, far_cut, shard):
    _, _, rows, width = inputs.shape
    ff = w_gate.shape[3]
    half = len(cut) // 2
    outs = [(rows, 2 * ff)] + [(half, ff, shard)] * 3 + [(rows, width)] * 2
    held = (inputs, w_gate, w_up, cotangent, w_down, cotangent, w_gate, w_up)
    vmem = pl.BlockSpec(memory_space=pltpu.VMEM)
    return pl.pallas_call(
        functools.partial(rest_kernel, cut, far_cut),
        out_shape=tuple(jax.ShapeDtypeStruct(dims, BF16) for dims in outs),
        in_specs=[pl.BlockSpec(memory_space=pltpu.SMEM)] + [pl.BlockSpec(memory_space=pl.ANY)] * 5 + [vmem] * 2,
        out_specs=[vmem] * len(outs),
        scratch_shapes=[pltpu.VMEM(array.shape[2:], BF16) for array in held] + [pltpu.SemaphoreType.DMA((8,))],
        compiler_params=pltpu.CompilerParams(vmem_limit_bytes=REST_LIMIT),
        cost_estimate=LONG,
        name="rest",
    )(mine, inputs, cotangent, w_gate, w_up, w_down, dgu1, hidden1)


def pair_kernel(mine, x0_ref, x1_ref, d0_ref, d1_ref, *outs):
    ff = outs[0].shape[1]
    x0, x1 = x0_ref[0, 0], x1_ref[0]
    d1 = jnp.concatenate([d1_ref[i] for i in range(d1_ref.shape[0])], axis=1)
    for i, out in enumerate(outs):
        part = slice(i * ff, (i + 1) * ff)
        out[0] = (rows_dot(d0_ref[:, part], x0) + rows_dot(d1[:, part], x1)).astype(BF16)


def pair(mine, inputs, mirrored_x, dgu, message, offsets, shard):
    _, _, rows, _ = inputs.shape
    both = dgu.shape[1]
    ff = both // 2
    count = len(offsets)

    def column(j, z):
        offset = sum(jnp.where(j == i, o, 0) for i, o in enumerate(offsets))
        return (0, 0, 0, z[0] ^ offset)

    pieces = both // shard
    return pl.pallas_call(
        pair_kernel,
        out_shape=(jax.ShapeDtypeStruct((count, ff, shard), BF16),) * 2,
        grid_spec=pltpu.PrefetchScalarGridSpec(
            num_scalar_prefetch=1,
            grid=(count,),
            in_specs=[
                pl.BlockSpec((1, 1, rows, shard), column),
                pl.BlockSpec((1, rows, shard), lambda j, z: (j, 0, 0)),
                pl.BlockSpec((rows, both), lambda j, z: (0, 0)),
                pl.BlockSpec((pieces, rows, shard), lambda j, z: (count // pieces, 0, 0)),
            ],
            out_specs=[pl.BlockSpec((1, ff, shard), lambda j, z: (j, 0, 0))] * 2,
        ),
        compiler_params=pltpu.CompilerParams(vmem_limit_bytes=VMEM_LIMIT),
        cost_estimate=LONG,
        name="pair",
    )(mine, inputs, mirrored_x, dgu, message)


def momentum_kernel(scale, count, *refs):
    moms, parts, outs = refs[:count], refs[count:-count], refs[-count:]
    ff = moms[0].shape[2]
    for i in range(count):
        total = parts[0][0, i * ff : (i + 1) * ff].astype(F32)
        for ref in parts[1:]:
            total = total + ref[0, i * ff : (i + 1) * ff].astype(F32)
        outs[i][0] = 0.9 * moms[i][0] + total.T * scale


def momentum(moms, parts, scale):
    shape = moms[0].shape
    _, shard, ff = shape
    count = len(moms)
    step = shard // 2 if shard % 256 == 0 else shard
    whole = pl.BlockSpec((1, step, ff), lambda i: (0, i, 0))
    return pl.pallas_call(
        functools.partial(momentum_kernel, scale, count),
        out_shape=(jax.ShapeDtypeStruct(shape, F32),) * count,
        grid=(shard // step,),
        in_specs=[whole] * count + [pl.BlockSpec((1, ff * count, step), lambda i: (0, 0, i))] * len(parts),
        out_specs=[whole] * count,
        compiler_params=pltpu.CompilerParams(vmem_limit_bytes=2 * VMEM_LIMIT),
        cost_estimate=COST,
        name="momentum",
    )(*moms, *parts)


def shifted(value, steps, name):
    count = lax.axis_size("section")
    first, last = max(0, -steps), min(count, count - steps)
    with jax.named_scope(name):
        return lax.ppermute(value, "section", [(i, i + steps) for i in range(first, last)])


def mirrored(value, name):
    count = lax.axis_size("section")
    with jax.named_scope(name):
        return lax.ppermute(value, "section", [(i, count - 1 - i) for i in range(count)])


def swapped(value, mask, name):
    with jax.named_scope(name):
        return lax.ppermute(value, "dp", [(i, i ^ mask) for i in range(lax.axis_size("dp"))])


def after(value, earlier):
    return lax.optimization_barrier((value, earlier))[0]


def add(left, right):
    return (left.astype(F32) + right.astype(F32)).astype(BF16)


def halve(keep, received):
    (stay, go), (stayed, gone) = (jnp.split(v, 2, -3) for v in (keep, received))
    return add(stay, stayed), add(go, gone)


def join_kernel(first_ref, second_ref, out_ref):
    out_ref[0, 0] = first_ref[...]
    out_ref[0, 1] = second_ref[...]


def join(first, second):
    rows, width = first.shape
    step = min(64, rows)
    return pl.pallas_call(
        join_kernel,
        out_shape=jax.ShapeDtypeStruct((1, 2, rows, width), first.dtype),
        grid=(rows // step,),
        in_specs=[pl.BlockSpec((step, width), lambda i: (i, 0))] * 2,
        out_specs=pl.BlockSpec((1, 2, step, width), lambda i: (0, 0, i, 0)),
        compiler_params=pltpu.CompilerParams(vmem_limit_bytes=VMEM_LIMIT),
        cost_estimate=LONG,
        name="join",
    )(first, second)


def body(inputs, cotangent, w_gate, w_up, w_down, mom_gate, mom_up, mom_down):
    replicas = lax.axis_size("dp")
    _, _, rows, width = inputs.shape
    shard = width // replicas
    half = replicas // 2
    masks = [1 << i for i in range(replicas.bit_length() - 1)]
    cut = slot_offsets(replicas, masks)
    mine = lax.axis_index("dp")[None]
    scale = 1.0 / math.sqrt(rows * replicas)

    operands = (mine, inputs, cotangent, w_gate, w_up, w_down)

    dgu1, hidden1, send1, message, x_keep = second(*operands, cut, cut, shard)
    message = mirrored(message, "message")
    first1 = swapped(send1, masks[0], "down1_first")
    x_keep = mirrored(x_keep, "x_keep")
    dgu0, send0, keep0, keep1, dx0, dx1 = rest(*operands, dgu1, hidden1, cut, cut, shard)
    first0 = swapped(send0, masks[0], "down0_first")
    for mask in masks[1:]:
        keep1, send1 = halve(keep1, first1)
        first1 = swapped(send1, mask, "down1_rest")
    gate_send, up_send = pair(mine, inputs, message, after(dgu0, send1), message, cut[half:], shard)
    gate = swapped(gate_send, masks[0], "gate_first")
    up = swapped(up_send, masks[0], "up_first")
    gate_first = gate
    recv0 = shifted(after(dx0, gate_send), -1, "dx_first")
    recv1 = shifted(after(dx1, gate_send), 1, "dx_second")
    grad_in = join(recv0, recv1)
    gate_keep, up_keep = pair(mine, inputs, x_keep, dgu0, message, cut[:half], shard)
    for mask in masks[1:]:
        keep0, send = halve(keep0, first0)
        first0 = swapped(send, mask, "down0_rest")
    for mask in masks[1:]:
        gate_keep, send = halve(gate_keep, gate)
        gate = swapped(after(send, first0), mask, "gate_rest")
    for mask in masks[1:]:
        up_keep, send = halve(up_keep, up)
        up = swapped(send, mask, "up_rest")
    mirror = mirrored(after(add(keep1, first1), gate_first), "down_mirror")
    new_up = momentum([mom_up], (up_keep, up), scale)
    new_down = momentum([mom_down], (keep0, first0, mirror), scale)
    new_gate = momentum([after(mom_gate, (new_down, grad_in))], (gate_keep, gate), scale)
    return (grad_in, *new_gate, *new_up, *new_down)


def solution(mesh):
    tokens = P("section", None, "dp", None)
    weights = P("section", None, None, None)
    moments = P("section", "dp", None)
    return jax.shard_map(
        body,
        mesh=mesh,
        in_specs=(tokens, tokens, weights, weights, weights, moments, moments, moments),
        out_specs=(tokens, moments, moments, moments),
        check_vma=False,
    )
```
